32 devices in a mesh: region: 2 (over x), blk: 8 (over z, y), rep: 2 (over core).
Axes of the slice: x: 2, y: 2, z: 4, core: 2. Of those that a mesh axis runs over, the one named last changes fastest.
Arguments:
- readings: bfloat16 [2, 65536, 896], P(None, ('region', 'blk', 'rep')), parts along dimension 1, may hold values from -6 to 6
- tile_mask: int32 [2, 512, 7], P(None, ('region', 'blk', 'rep')), parts along dimension 1, may hold values from 0 to 1, as said below
- sys_factors: float32 [65536, 128], P(('region', 'blk', 'rep')), parts along dimension 0, may hold values from -2 to 2
- sys_first: float32 [65536, 128], P(('region', 'blk', 'rep')), parts along dimension 0, may hold values from -20 to 20
- sys_second: float32 [65536, 128], P(('region', 'blk', 'rep')), parts along dimension 0, may hold values from 10 to 400
- time_factors: float32 [14336, 128], P(('region', 'blk')), parts along dimension 0, may hold values from -2 to 2
- time_first: float32 [14336, 128], P(('region', 'blk')), parts along dimension 0, may hold values from -30 to 30
- time_second: float32 [14336, 128], P(('region', 'blk')), parts along dimension 0, may hold values from 20 to 800
Outputs:
- sys_out: float32 [65536, 128], P(('region', 'blk', 'rep')), parts along dimension 0
- time_out: float32 [14336, 128], P(('region', 'blk')), parts along dimension 0
The draws below stay inside these ranges and needn't reach their ends.
There are 2 independent parts, one for each index of `region`. The reference program is written for one: setup_inputs(seed, part) draws one part's arguments, and reference() takes and returns one part's arrays. A program takes and returns all parts, laid end to end along the dimension named above; each array names one. Nothing has to cross between parts.
Inputs may be any that keep to these rules, and one draw needn't show every extreme that they name: `tile_mask`: 1 where the tile of 128 systems by 128 quarter-hours is observed, else 0.
All inputs are finite; a program needn't handle non-finite values.
Results may differ from the reference program's by a relative error of at most 0.0003.
Values sent between devices are 32-bit elements; how exact they have to be, the bound alone decides.
A program may use at most 128 MiB of HBM per device.

```python
import math
import jax
import jax.numpy as jnp
from jax import lax

RANK = 128
TILE = 128
SUB = 2
SYS_DEV = 2048
TB = 896
SYSTEMS = 32768
TIME = 7168
N_BLK = 8
N_REP = 2


def draw_tile_mask(key, part):
    level_key = jax.random.fold_in(key, 11)
    tile_key = jax.random.fold_in(key, 23)
    levels = jax.random.randint(level_key, (SYSTEMS // TILE,), 0, 5)
    tiles = jax.random.randint(tile_key, (SUB, SYSTEMS // TILE, TB // TILE), 0, 4)
    return (tiles < levels[None, :, None]).astype(jnp.int32)


def block_levels(stream_key, shape, shards, smallest, top_value):
    factor_of, own = 1.0, jax.random.fold_in(stream_key, 6)
    for position, blocks in shards:
        heights = jnp.exp(jax.random.uniform(jax.random.fold_in(own, position), (blocks,), jnp.float32, smallest / len(shards), top_value / len(shards)))
        factor_of = factor_of * jnp.repeat(heights, shape[position] // blocks).reshape([-1 if axis == position else 1 for axis in range(len(shape))])
    return factor_of


def bell_draw(key, shape, width, reach, shards=(), dtype=jnp.bfloat16):
    drawn = jax.random.normal(key, shape, jnp.float32) * width
    if len(shards) > 0:
        drawn = block_levels(key, shape, shards, -0.22, 0.18) * drawn
    return jnp.clip(drawn, min=-reach, max=reach).astype(dtype)


def setup_inputs(seed: int = 0, part: int = 0) -> dict:
    key_list = jax.random.split(jax.random.key(seed), 9)
    own_keys = jax.random.split(jax.random.fold_in(key_list[8], part), 9)
    readings = bell_draw(own_keys[0], (SUB, SYSTEMS, TB), 1.0, 6.0, ((1, 16),))
    tile_mask = draw_tile_mask(jax.random.fold_in(jax.random.fold_in(key_list[8], part), 71), part)
    sys_factors = bell_draw(own_keys[2], (SYSTEMS, RANK), 0.3, 2.0, ((0, 16),), jnp.float32)
    sys_first = bell_draw(own_keys[3], (SYSTEMS, RANK), 3.0, 20.0, ((0, 16),), jnp.float32)
    sys_second = jnp.clip(jnp.exp(math.log(400.0) - 3.6888795 * jax.random.uniform(own_keys[4], (SYSTEMS, RANK), jnp.float32) ** block_levels(own_keys[4], (SYSTEMS, RANK), ((0, 16),), -0.2, 0.2)), 10.0, 400.0)
    time_factors = bell_draw(own_keys[5], (TIME, RANK), 0.3, 2.0, ((0, 8),), jnp.float32)
    time_first = bell_draw(own_keys[6], (TIME, RANK), 5.0, 30.0, ((0, 8),), jnp.float32)
    time_second = jnp.clip(jnp.exp(math.log(800.0) - 3.6888795 * jax.random.uniform(own_keys[7], (TIME, RANK), jnp.float32) ** block_levels(own_keys[7], (TIME, RANK), ((0, 8),), -0.2, 0.2)), 20.0, 800.0)
    return dict(readings=readings, tile_mask=tile_mask, sys_factors=sys_factors, sys_first=sys_first, sys_second=sys_second, time_factors=time_factors, time_first=time_first, time_second=time_second)


learn_rate = 0.1
beta_one = 0.8
beta_two = 0.99
adam_eps = 1e-08
decay_weight = 0.01

def adam_step(param, first, second, grad):
    first_new = beta_one * first + (1.0 - beta_one) * grad
    second_new = beta_two * second + (1.0 - beta_two) * grad * grad
    param_new = param - learn_rate * first_new / (jnp.sqrt(second_new) + adam_eps)
    return (param_new, first_new, second_new)

def residual_grads(sys_rows, time_rows, data, observed):
    sys_low = sys_rows.astype(jnp.bfloat16)
    time_low = time_rows.astype(jnp.bfloat16)
    predict = jnp.dot(sys_low, time_low.T, preferred_element_type=jnp.float32)
    rows, cols = predict.shape
    keep = observed.astype(jnp.float32)[:, None, :, None]
    diff = (predict - data.astype(jnp.float32)).reshape(rows // TILE, TILE, cols // TILE, TILE) * keep
    error = diff.reshape(rows, cols).astype(jnp.bfloat16)
    grad_sys = jnp.dot(error, time_low, preferred_element_type=jnp.float32)
    grad_time = lax.dot_general(error, sys_low, (((0,), (0,)), ((), ())), preferred_element_type=jnp.float32)
    return (grad_sys, grad_time)

def reference(readings, tile_mask, sys_factors, sys_first, sys_second, time_factors, time_first, time_second):
    shard_rows = SYS_DEV * N_REP
    sys_rows = sys_factors.reshape(N_BLK, shard_rows, RANK)
    sys_one = sys_first.reshape(N_BLK, shard_rows, RANK)
    sys_two = sys_second.reshape(N_BLK, shard_rows, RANK)
    held = time_factors.reshape(N_BLK, TB, RANK)
    held_one = time_first.reshape(N_BLK, TB, RANK)
    held_two = time_second.reshape(N_BLK, TB, RANK)
    for step in range(SUB):
        data = readings[step].reshape(N_BLK, shard_rows, TB)
        observed = tile_mask[step].reshape(N_BLK, shard_rows // TILE, TB // TILE)

        def shard_grads(items):
            return residual_grads(items[0], items[1], items[2], items[3])
        grad_sys, grad_time = lax.map(shard_grads, (sys_rows, held, data, observed))
        sys_rows, sys_one, sys_two = adam_step(sys_rows, sys_one, sys_two, grad_sys + decay_weight * sys_rows)
        held, held_one, held_two = adam_step(held, held_one, held_two, grad_time + decay_weight * held)
        held = jnp.roll(held, 1, axis=0)
        held_one = jnp.roll(held_one, 1, axis=0)
        held_two = jnp.roll(held_two, 1, axis=0)
    return (sys_rows.reshape(SYSTEMS, RANK), held.reshape(TIME, RANK))
```

```python
import functools

import jax
import jax.numpy as jnp
from jax import lax
from jax.experimental import pallas as pl
from jax.experimental.pallas import tpu as pltpu
from jax.sharding import PartitionSpec as P

TILE = 128
CHUNK = 256
ROWS = 256
MESH = pl.DeviceIdType.MESH

learn_rate = 0.1
beta_one = 0.8
beta_two = 0.99
adam_eps = 1e-08
decay_weight = 0.01


def adam_step(param, first, second, grad):
    first_new = beta_one * first + (1.0 - beta_one) * grad
    second_new = beta_two * second + (1.0 - beta_two) * grad * grad
    param_new = param - learn_rate * first_new / (jnp.sqrt(second_new) + adam_eps)
    return (param_new, first_new, second_new)


def kernel(
    n_blk, chunks,
    data_hbm, mask_ref, u_hbm, um_hbm, uv_hbm, h_hbm, hm_hbm, hv_hbm,
    u_out, h_out,
    data, u, um, uv, ub, err, h, hm, hv, hn, hb, part, px, gb, gr, mx, h2,
    in_sem, data_sem, out_sem,
    x_send, x_recv, h_send, h_recv, f_send, f_recv, g_send, g_recv,
    m_send, m_recv, o_send, o_recv, p_send, p_recv, q_send, q_recv,
):
    systems = u.shape[0]
    count = len(chunks)
    last = count - 1
    me = lax.axis_index("blk")
    core = lax.axis_index("rep")
    other = 1 - core
    after, before = lax.rem(me + 1, n_blk), lax.rem(me + n_blk - 1, n_blk)
    after2, before2 = lax.rem(me + 2, n_blk), lax.rem(me + n_blk - 2, n_blk)

    barrier = pltpu.get_barrier_semaphore()
    friends = [
        {"rep": other},
        {"blk": after}, {"blk": after, "rep": other},
        {"blk": before}, {"blk": before, "rep": other},
        {"blk": after2}, {"blk": before2},
    ]
    for friend in friends:
        pl.semaphore_signal(barrier, inc=1, device_id=friend, device_id_type=MESH)

    def fetch(src, dst, k):
        return pltpu.make_async_copy(src, dst, in_sem.at[k])

    in_h, in_u = fetch(h_hbm, h, 0), fetch(u_hbm, u, 1)
    in_hm, in_hv = fetch(hm_hbm, hm, 2), fetch(hv_hbm, hv, 3)
    in_um, in_uv = fetch(um_hbm, um, 4), fetch(uv_hbm, uv, 5)
    in_data = [
        [
            pltpu.make_async_copy(
                data_hbm.at[s, :, pl.ds(off, w)], data.at[s, :, pl.ds(off, w)], data_sem.at[s, c]
            )
            for c, (off, w) in enumerate(chunks)
        ]
        for s in range(2)
    ]
    in_h.start()
    in_u.start()
    for c in range(count):
        in_data[0][c].start()
        if c == 0:
            in_hm.start()
            in_hv.start()
    in_um.start()
    in_uv.start()
    for c in range(count):
        in_data[1][c].start()

    def remote(src, dst, send, recv, device):
        return pltpu.make_async_remote_copy(
            src_ref=src, dst_ref=dst, send_sem=send, recv_sem=recv,
            device_id=device, device_id_type=MESH,
        )

    def rows_of(c, which):
        off, w = chunks[c]
        return pl.ds(pl.multiple_of(off + which * (w // 2), w // 2), w // 2)

    def half_of(c):
        off, w = chunks[c]
        return pl.ds(off // 2, w // 2)

    swap = [
        [
            remote(part.at[s, rows_of(c, other)], px.at[s, half_of(c)],
                   x_send.at[s, c], x_recv.at[s, c], {"rep": other})
            for c in range(count)
        ]
        for s in range(2)
    ]
    pass_h = [
        remote(h.at[rows_of(c, core)], hn.at[rows_of(c, core)], h_send.at[c], h_recv.at[c], {"blk": after})
        for c in range(count)
    ]
    share_h = [
        remote(hn.at[rows_of(c, core)], hn.at[rows_of(c, core)], f_send.at[c], f_recv.at[c], {"rep": other})
        for c in range(count)
    ]
    back = [
        remote(gb.at[half_of(c)], gr.at[half_of(c)], g_send.at[c], g_recv.at[c], {"blk": before})
        for c in range(last)
    ]
    final = [
        remote(h2.at[half_of(c)], h_out.at[rows_of(c, core)], o_send.at[c], o_recv.at[c],
               {"blk": after if c == last else after2})
        for c in range(count)
    ]
    share_out = [
        remote(h_out.at[rows_of(c, core)], h_out.at[rows_of(c, core)], p_send.at[c], p_recv.at[c], {"rep": other})
        for c in range(last)
    ]
    final_two = remote(
        h2.at[half_of(last)], h_out.at[rows_of(last, core)], q_send, q_recv, {"blk": after, "rep": other}
    )
    pass_m = [
        remote(src.at[rows_of(last, core)], mx.at[k], m_send.at[k], m_recv.at[k], {"blk": after})
        for k, src in enumerate((hm, hv))
    ]

    def grads(s, c):
        off, w = chunks[c]

        def block(i):
            rows = pl.ds(pl.multiple_of(i * ROWS, ROWS), ROWS)
            predict = lax.dot_general(
                ub[rows, :], hb[off : off + w, :], (((1,), (1,)), ((), ())),
                preferred_element_type=jnp.float32,
            )
            diff = predict - data[s, rows, off : off + w].astype(jnp.float32)
            for a in range(ROWS // TILE):
                for b in range(w // TILE):
                    keep = mask_ref[s, i * (ROWS // TILE) + a, off // TILE + b].astype(jnp.float32)
                    piece = diff[a * TILE : (a + 1) * TILE, b * TILE : (b + 1) * TILE] * keep
                    err[
                        pl.ds(pl.multiple_of(i * ROWS + a * TILE, TILE), TILE),
                        off + b * TILE : off + (b + 1) * TILE,
                    ] = piece.astype(jnp.bfloat16)

        def pair(i, carry):
            block(2 * i)
            block(2 * i + 1)
            return carry

        lax.fori_loop(0, systems // ROWS // 2, pair, 0)
        part[s, off : off + w, :] = lax.dot_general(
            err[:, off : off + w], ub[...], (((0,), (0,)), ((), ())),
            preferred_element_type=jnp.float32,
        )

    def sys_block(s, i):
        rows = pl.ds(pl.multiple_of(i * ROWS, ROWS), ROWS)
        grad = jnp.dot(err[rows, :], hb[...], preferred_element_type=jnp.float32)
        param = u[rows, :]
        new, one, two = adam_step(param, um[rows, :], uv[rows, :], grad + decay_weight * param)
        u[rows, :] = new
        if s == 0:
            um[rows, :] = one
            uv[rows, :] = two
            ub[rows, :] = new.astype(jnp.bfloat16)

    pieces = 4
    per = systems // pieces

    def sys_piece(s, p):
        for i in range(p * per // ROWS, (p + 1) * per // ROWS):
            sys_block(s, i)

    out_copy = [
        pltpu.make_async_copy(u.at[pl.ds(p * per, per)], u_out.at[pl.ds(p * per, per)], out_sem.at[p])
        for p in range(pieces)
    ]

    def home_first(c):
        swap[0][c].wait_recv()
        rows = rows_of(c, core)
        param = h[rows, :]
        grad = part[0, rows, :] + px[0, half_of(c), :] + decay_weight * param
        new, one, two = adam_step(param, hm[rows, :], hv[rows, :], grad)
        h[rows, :] = new
        hm[rows, :] = one
        hv[rows, :] = two
        pass_h[c].start()
        if c == last:
            for copy in pass_m:
                copy.start()

    def hand_on(c):
        pass_h[c].wait_recv()
        share_h[c].start()

    def give_back(c):
        swap[1][c].wait_recv()
        rows = rows_of(c, core)
        gb[half_of(c), :] = part[1, rows, :] + px[1, half_of(c), :]
        back[c].start()

    def home_second(c):
        back[c].wait_recv()
        rows = rows_of(c, core)
        param = h[rows, :]
        grad = gr[half_of(c), :] + decay_weight * param
        h2[half_of(c), :] = adam_step(param, hm[rows, :], hv[rows, :], grad)[0]
        final[c].start()

    def finish_last():
        for copy in pass_m:
            copy.wait_recv()
        swap[1][last].wait_recv()
        rows = rows_of(last, core)
        param = hn[rows, :]
        grad = part[1, rows, :] + px[1, half_of(last), :] + decay_weight * param
        h2[half_of(last), :] = adam_step(param, mx[0], mx[1], grad)[0]
        final[last].start()
        final_two.start()

    def share_final(c):
        final[c].wait_recv()
        share_out[c].start()

    in_h.wait()
    hb[...] = h[...].astype(jnp.bfloat16)
    in_u.wait()
    ub[...] = u[...].astype(jnp.bfloat16)
    for c in range(count):
        in_data[0][c].wait()
        grads(0, c)
        if c == 0:
            pl.semaphore_wait(barrier, len(friends))
            in_hm.wait()
            in_hv.wait()
        swap[0][c].start()
        if c >= 1:
            home_first(c - 1)
    in_um.wait()
    in_uv.wait()
    sys_piece(0, 0)
    home_first(last)
    for p in range(1, pieces):
        hand_on(p - 1)
        sys_piece(0, p)
    for c in range(pieces - 1, count):
        hand_on(c)

    for c, (off, w) in enumerate(chunks):
        in_data[1][c].wait()
        share_h[c].wait_recv()
        hb[off : off + w, :] = hn[off : off + w, :].astype(jnp.bfloat16)
        grads(1, c)
        swap[1][c].start()
        if c >= 1:
            give_back(c - 1)
        if c >= 2:
            home_second(c - 2)
    sys_piece(1, 0)
    out_copy[0].start()
    finish_last()
    home_second(last - 1)
    for p in range(1, pieces):
        sys_piece(1, p)
        out_copy[p].start()
        if p <= last:
            share_final(p - 1)
    for c in range(pieces - 1, last):
        share_final(c)

    for s in range(2):
        for c in range(count):
            swap[s][c].wait_send()
    for group in (pass_h, share_h, back, final, share_out, pass_m, [final_two]):
        for copy in group:
            copy.wait_send()
    for copy in share_out:
        copy.wait_recv()
    final[last].wait_recv()
    final_two.wait_recv()
    for copy in out_copy:
        copy.wait()


def on_device(
    readings, tile_mask, sys_factors, sys_first, sys_second, time_factors, time_first, time_second
):
    n_blk = lax.axis_size("blk")
    systems, rank = sys_factors.shape
    times = time_factors.shape[0]
    chunks = tuple((off, min(CHUNK, times - off)) for off in range(0, times, CHUNK))
    count = len(chunks)
    f32, bf16 = jnp.float32, jnp.bfloat16
    dma = pltpu.SemaphoreType.DMA
    anywhere = pl.BlockSpec(memory_space=pl.ANY)
    small = chunks[-1][1] // 2
    return pl.pallas_call(
        functools.partial(kernel, n_blk, chunks),
        out_shape=(
            jax.ShapeDtypeStruct((systems, rank), f32),
            jax.ShapeDtypeStruct((times, rank), f32),
        ),
        in_specs=[anywhere, pl.BlockSpec(memory_space=pltpu.SMEM)] + [anywhere] * 6,
        out_specs=(anywhere, anywhere),
        scratch_shapes=[
            pltpu.VMEM((2, systems, times), bf16),
            pltpu.VMEM((systems, rank), f32),
            pltpu.VMEM((systems, rank), f32),
            pltpu.VMEM((systems, rank), f32),
            pltpu.VMEM((systems, rank), bf16),
            pltpu.VMEM((systems, times), bf16),
            pltpu.VMEM((times, rank), f32),
            pltpu.VMEM((times, rank), f32),
            pltpu.VMEM((times, rank), f32),
            pltpu.VMEM((times, rank), f32),
            pltpu.VMEM((times, rank), bf16),
            pltpu.VMEM((2, times, rank), f32),
            pltpu.VMEM((2, times // 2, rank), f32),
            pltpu.VMEM((times // 2, rank), f32),
            pltpu.VMEM((times // 2, rank), f32),
            pltpu.VMEM((2, small, rank), f32),
            pltpu.VMEM((times // 2, rank), f32),
            dma((6,)), dma((2, count)), dma((4,)),
            dma((2, count)), dma((2, count)),
            dma((count,)), dma((count,)),
            dma((count,)), dma((count,)),
            dma((count,)), dma((count,)),
            dma((2,)), dma((2,)),
            dma((count,)), dma((count,)),
            dma((count,)), dma((count,)),
            dma, dma,
        ],
        compiler_params=pltpu.CompilerParams(
            collective_id=0, has_side_effects=True, vmem_limit_bytes=56 * 1024 * 1024
        ),
    )(readings, tile_mask, sys_factors, sys_first, sys_second, time_factors, time_first, time_second)


def solution(mesh):
    return jax.shard_map(
        on_device,
        mesh=mesh,
        in_specs=(
            P(None, ("region", "blk", "rep"), None),
            P(None, ("region", "blk", "rep"), None),
            P(("region", "blk", "rep"), None),
            P(("region", "blk", "rep"), None),
            P(("region", "blk", "rep"), None),
            P(("region", "blk"), None),
            P(("region", "blk"), None),
            P(("region", "blk"), None),
        ),
        out_specs=(P(("region", "blk", "rep"), None), P(("region", "blk"), None)),
        check_vma=False,
    )
```

```python
import functools

import jax
import jax.numpy as jnp
from jax import lax
from jax.experimental import pallas as pl
from jax.experimental.pallas import tpu as pltpu
from jax.sharding import PartitionSpec as P

TILE = 128
CHUNK = 256
HOME = ()
ROWS = 256
MESH = pl.DeviceIdType.MESH

learn_rate = 0.1
beta_one = 0.8
beta_two = 0.99
adam_eps = 1e-08
decay_weight = 0.01


def adam_step(param, first, second, grad):
    first_new = beta_one * first + (1.0 - beta_one) * grad
    second_new = beta_two * second + (1.0 - beta_two) * grad * grad
    param_new = param - learn_rate * first_new / (jnp.sqrt(second_new) + adam_eps)
    return (param_new, first_new, second_new)


def kernel(
    n_blk, chunks,
    data_hbm, mask_ref, u_hbm, um_hbm, uv_hbm, h_hbm, hm_hbm, hv_hbm,
    u_out, h_out,
    data, u, um, uv, ub, err, h, hm, hv, hn, hb, part, px, gb, gr, mx, h2, ho,
    in_sem, data_sem, out_sem, ho_sem,
    x_send, x_recv, h_send, h_recv, f_send, f_recv, g_send, g_recv,
    m_send, m_recv, o_send, o_recv, p_send, p_recv, q_send, q_recv,
):
    systems = u.shape[0]
    count = len(chunks)
    last = count - 1
    me = lax.axis_index("blk")
    core = lax.axis_index("rep")
    other = 1 - core
    after, before = lax.rem(me + 1, n_blk), lax.rem(me + n_blk - 1, n_blk)
    after2, before2 = lax.rem(me + 2, n_blk), lax.rem(me + n_blk - 2, n_blk)

    barrier = pltpu.get_barrier_semaphore()
    friends = [
        {"rep": other},
        {"blk": after}, {"blk": after, "rep": other},
        {"blk": before}, {"blk": before, "rep": other},
        {"blk": after2}, {"blk": before2},
    ]
    for friend in friends:
        pl.semaphore_signal(barrier, inc=1, device_id=friend, device_id_type=MESH)

    def fetch(src, dst, k):
        return pltpu.make_async_copy(src, dst, in_sem.at[k])

    in_h, in_u = fetch(h_hbm, h, 0), fetch(u_hbm, u, 1)
    in_hm, in_hv = fetch(hm_hbm, hm, 2), fetch(hv_hbm, hv, 3)
    in_um, in_uv = fetch(um_hbm, um, 4), fetch(uv_hbm, uv, 5)
    in_data = [
        [
            pltpu.make_async_copy(
                data_hbm.at[s, :, pl.ds(off, w)], data.at[s, :, pl.ds(off, w)], data_sem.at[s, c]
            )
            for c, (off, w) in enumerate(chunks)
        ]
        for s in range(2)
    ]
    in_h.start()
    in_u.start()
    for c in range(count):
        in_data[0][c].start()
        if c == 0:
            in_hm.start()
            in_hv.start()
    in_um.start()
    in_uv.start()
    for c in range(count):
        in_data[1][c].start()

    def remote(src, dst, send, recv, device):
        return pltpu.make_async_remote_copy(
            src_ref=src, dst_ref=dst, send_sem=send, recv_sem=recv,
            device_id=device, device_id_type=MESH,
        )

    def rows_of(c, which):
        off, w = chunks[c]
        return pl.ds(pl.multiple_of(off + which * (w // 2), w // 2), w // 2)

    def half_of(c):
        off, w = chunks[c]
        return pl.ds(off // 2, w // 2)

    swap = [
        [
            remote(part.at[s, rows_of(c, other)], px.at[s, half_of(c)],
                   x_send.at[s, c], x_recv.at[s, c], {"rep": other})
            for c in range(count)
        ]
        for s in range(2)
    ]
    pass_h = [
        remote(h.at[rows_of(c, core)], hn.at[rows_of(c, core)], h_send.at[c], h_recv.at[c], {"blk": after})
        for c in range(count)
    ]
    share_h = [
        remote(hn.at[rows_of(c, core)], hn.at[rows_of(c, core)], f_send.at[c], f_recv.at[c], {"rep": other})
        for c in range(count)
    ]
    back = [
        remote(gb.at[half_of(c)], gr.at[half_of(c)], g_send.at[c], g_recv.at[c], {"blk": before})
        for c in range(count)
    ]
    final = [
        remote(h2.at[half_of(c)], (h_out if c == last else ho).at[rows_of(c, core)], o_send.at[c], o_recv.at[c],
               {"blk": after2 if c in HOME else after})
        for c in range(count)
    ]
    share_out = [
        remote(ho.at[rows_of(c, core)], ho.at[rows_of(c, core)], p_send.at[c], p_recv.at[c], {"rep": other})
        for c in range(last)
    ]
    final_two = remote(
        h2.at[half_of(last)], h_out.at[rows_of(last, core)], q_send, q_recv, {"blk": after, "rep": other}
    )
    pass_m = [
        [
            remote(src.at[rows_of(c, core)], mx.at[k, half_of(c)], m_send.at[k, c], m_recv.at[k, c], {"blk": after})
            for k, src in enumerate((hm, hv))
        ]
        for c in range(count)
    ]
    travel = [c for c in range(count) if c not in HOME]

    def grads(s, c):
        off, w = chunks[c]

        def block(i):
            rows = pl.ds(pl.multiple_of(i * ROWS, ROWS), ROWS)
            predict = lax.dot_general(
                ub[rows, :], hb[off : off + w, :], (((1,), (1,)), ((), ())),
                preferred_element_type=jnp.float32,
            )
            diff = predict - data[s, rows, off : off + w].astype(jnp.float32)
            for a in range(ROWS // TILE):
                for b in range(w // TILE):
                    keep = mask_ref[off // TILE + b, s, i * (ROWS // TILE) + a].astype(jnp.float32)
                    piece = diff[a * TILE : (a + 1) * TILE, b * TILE : (b + 1) * TILE] * keep
                    err[
                        pl.ds(pl.multiple_of(i * ROWS + a * TILE, TILE), TILE),
                        off + b * TILE : off + (b + 1) * TILE,
                    ] = piece.astype(jnp.bfloat16)

        def pair(i, carry):
            block(2 * i)
            block(2 * i + 1)
            return carry

        lax.fori_loop(0, systems // ROWS // 2, pair, 0)
        part[s, off : off + w, :] = lax.dot_general(
            err[:, off : off + w], ub[...], (((0,), (0,)), ((), ())),
            preferred_element_type=jnp.float32,
        )

    def sys_block(s, i):
        rows = pl.ds(pl.multiple_of(i * ROWS, ROWS), ROWS)
        grad = jnp.dot(err[rows, :], hb[...], preferred_element_type=jnp.float32)
        param = u[rows, :]
        new, one, two = adam_step(param, um[rows, :], uv[rows, :], grad + decay_weight * param)
        u[rows, :] = new
        if s == 0:
            um[rows, :] = one
            uv[rows, :] = two
            ub[rows, :] = new.astype(jnp.bfloat16)

    pieces = 4
    per = systems // pieces

    def sys_piece(s, p):
        for i in range(p * per // ROWS, (p + 1) * per // ROWS):
            sys_block(s, i)

    out_copy = [
        pltpu.make_async_copy(u.at[pl.ds(p * per, per)], u_out.at[pl.ds(p * per, per)], out_sem.at[p])
        for p in range(pieces)
    ]

    ho_copy = [
        pltpu.make_async_copy(ho.at[pl.ds(off, w)], h_out.at[pl.ds(off, w)], ho_sem.at[c])
        for c, (off, w) in enumerate(chunks[:last])
    ]

    def home_first(c):
        swap[0][c].wait_recv()
        rows = rows_of(c, core)
        param = h[rows, :]
        grad = part[0, rows, :] + px[0, half_of(c), :] + decay_weight * param
        new, one, two = adam_step(param, hm[rows, :], hv[rows, :], grad)
        h[rows, :] = new
        hm[rows, :] = one
        hv[rows, :] = two
        pass_h[c].start()
        if c == last:
            for k in travel:
                for copy in pass_m[k]:
                    copy.start()

    def hand_on(c):
        pass_h[c].wait_recv()
        share_h[c].start()

    def give_back(c):
        swap[1][c].wait_recv()
        rows = rows_of(c, core)
        gb[half_of(c), :] = part[1, rows, :] + px[1, half_of(c), :]
        back[c].start()

    def home_second(c):
        back[c].wait_recv()
        rows = rows_of(c, core)
        param = h[rows, :]
        grad = gr[half_of(c), :] + decay_weight * param
        h2[half_of(c), :] = adam_step(param, hm[rows, :], hv[rows, :], grad)[0]
        final[c].start()

    def finish(c):
        for copy in pass_m[c]:
            copy.wait_recv()
        swap[1][c].wait_recv()
        rows = rows_of(c, core)
        param = hn[rows, :]
        grad = part[1, rows, :] + px[1, half_of(c), :] + decay_weight * param
        h2[half_of(c), :] = adam_step(param, mx[0, half_of(c), :], mx[1, half_of(c), :], grad)[0]
        final[c].start()
        if c == last:
            final_two.start()

    def share_final(c):
        final[c].wait_recv()
        share_out[c].start()

    in_h.wait()
    hb[...] = h[...].astype(jnp.bfloat16)
    in_u.wait()
    ub[...] = u[...].astype(jnp.bfloat16)
    for c in range(count):
        in_data[0][c].wait()
        grads(0, c)
        if c == 0:
            pl.semaphore_wait(barrier, len(friends))
            in_hm.wait()
            in_hv.wait()
        swap[0][c].start()
        if c >= 1:
            home_first(c - 1)
    in_um.wait()
    in_uv.wait()
    sys_piece(0, 0)
    home_first(last)
    for p in range(1, pieces):
        sys_piece(0, p)
    hand_on(0)

    for c, (off, w) in enumerate(chunks):
        if c < last:
            hand_on(c + 1)
        in_data[1][c].wait()
        share_h[c].wait_recv()
        hb[off : off + w, :] = hn[off : off + w, :].astype(jnp.bfloat16)
        grads(1, c)
        swap[1][c].start()
        if c >= 1:
            give_back(c - 1) if c - 1 in HOME else finish(c - 1)
    sys_piece(1, 0)
    out_copy[0].start()
    finish(last)
    for c in HOME:
        home_second(c)
    for p in range(1, pieces):
        sys_piece(1, p)
        out_copy[p].start()
    for c in range(last):
        share_final(c)

    for c in range(last):
        share_out[c].wait_recv()
        ho_copy[c].start()
    for s in range(2):
        for c in range(count):
            swap[s][c].wait_send()
    for group in (pass_h, share_h, final, share_out, [final_two]):
        for copy in group:
            copy.wait_send()
    for c in range(count):
        for copy in [back[c]] if c in HOME else pass_m[c]:
            copy.wait_send()
    final[last].wait_recv()
    final_two.wait_recv()
    for copy in out_copy + ho_copy:
        copy.wait()


def place_kernel(u_in, h_in, u_to, h_to, u_mid, h_mid, read_sem, write_sem):
    per = u_in.shape[0] // 4
    moves = [(h_in, h_mid, h_to, pl.ds(0, h_in.shape[0]))] + [
        (u_in, u_mid, u_to, pl.ds(k * per, per)) for k in range(4)
    ]
    reads = [
        pltpu.make_async_copy(src.at[rows], mid.at[rows], read_sem.at[k])
        for k, (src, mid, _, rows) in enumerate(moves)
    ]
    writes = [
        pltpu.make_async_copy(mid.at[rows], dst.at[rows], write_sem.at[k])
        for k, (_, mid, dst, rows) in enumerate(moves)
    ]
    for read in reads:
        read.start()
    for read, write in zip(reads, writes):
        read.wait()
        write.start()
    for write in writes:
        write.wait()


def placed(u, h):
    anywhere = pl.BlockSpec(memory_space=pl.ANY)
    return pl.pallas_call(
        place_kernel,
        out_shape=(jax.ShapeDtypeStruct(u.shape, u.dtype), jax.ShapeDtypeStruct(h.shape, h.dtype)),
        in_specs=[anywhere, anywhere],
        out_specs=(anywhere, anywhere),
        scratch_shapes=[
            pltpu.VMEM(u.shape, u.dtype), pltpu.VMEM(h.shape, h.dtype),
            pltpu.SemaphoreType.DMA((5,)), pltpu.SemaphoreType.DMA((5,)),
        ],
        compiler_params=pltpu.CompilerParams(vmem_limit_bytes=56 * 1024 * 1024),
    )(u, h)


def on_device(
    readings, tile_mask, sys_factors, sys_first, sys_second, time_factors, time_first, time_second
):
    n_blk = lax.axis_size("blk")
    systems, rank = sys_factors.shape
    times = time_factors.shape[0]
    chunks = tuple((off, min(CHUNK, times - off)) for off in range(0, times, CHUNK))
    count = len(chunks)
    f32, bf16 = jnp.float32, jnp.bfloat16
    dma = pltpu.SemaphoreType.DMA
    anywhere = pl.BlockSpec(memory_space=pl.ANY)
    results = pl.pallas_call(
        functools.partial(kernel, n_blk, chunks),
        out_shape=(
            jax.ShapeDtypeStruct((systems, rank), f32),
            jax.ShapeDtypeStruct((times, rank), f32),
        ),
        in_specs=[anywhere, pl.BlockSpec(memory_space=pltpu.SMEM)] + [anywhere] * 6,
        out_specs=(anywhere, anywhere),
        scratch_shapes=[
            pltpu.VMEM((2, systems, times), bf16),
            pltpu.VMEM((systems, rank), f32),
            pltpu.VMEM((systems, rank), f32),
            pltpu.VMEM((systems, rank), f32),
            pltpu.VMEM((systems, rank), bf16),
            pltpu.VMEM((systems, times), bf16),
            pltpu.VMEM((times, rank), f32),
            pltpu.VMEM((times, rank), f32),
            pltpu.VMEM((times, rank), f32),
            pltpu.VMEM((times, rank), f32),
            pltpu.VMEM((times, rank), bf16),
            pltpu.VMEM((2, times, rank), f32),
            pltpu.VMEM((2, times // 2, rank), f32),
            pltpu.VMEM((times // 2, rank), f32),
            pltpu.VMEM((times // 2, rank), f32),
            pltpu.VMEM((2, times // 2, rank), f32),
            pltpu.VMEM((times // 2, rank), f32),
            pltpu.VMEM((times, rank), f32),
            dma((6,)), dma((2, count)), dma((4,)), dma((count,)),
            dma((2, count)), dma((2, count)),
            dma((count,)), dma((count,)),
            dma((count,)), dma((count,)),
            dma((count,)), dma((count,)),
            dma((2, count)), dma((2, count)),
            dma((count,)), dma((count,)),
            dma((count,)), dma((count,)),
            dma, dma,
        ],
        compiler_params=pltpu.CompilerParams(
            collective_id=0, has_side_effects=True, vmem_limit_bytes=56 * 1024 * 1024
        ),
    )(readings, jnp.transpose(tile_mask, (2, 0, 1)), sys_factors, sys_first, sys_second, time_factors, time_first, time_second)
    return placed(*results)


def solution(mesh):
    return jax.shard_map(
        on_device,
        mesh=mesh,
        in_specs=(
            P(None, ("region", "blk", "rep"), None),
            P(None, ("region", "blk", "rep"), None),
            P(("region", "blk", "rep"), None),
            P(("region", "blk", "rep"), None),
            P(("region", "blk", "rep"), None),
            P(("region", "blk"), None),
            P(("region", "blk"), None),
            P(("region", "blk"), None),
        ),
        out_specs=(P(("region", "blk", "rep"), None), P(("region", "blk"), None)),
        check_vma=False,
    )
```

```python
import functools

import jax
import jax.numpy as jnp
from jax import lax
from jax.experimental import pallas as pl
from jax.experimental.pallas import tpu as pltpu
from jax.sharding import PartitionSpec as P

TILE = 128
CHUNK = 256
HOME = ()
ROWS = 256
MESH = pl.DeviceIdType.MESH

learn_rate = 0.1
beta_one = 0.8
beta_two = 0.99
adam_eps = 1e-08
decay_weight = 0.01


def adam_step(param, first, second, grad):
    first_new = beta_one * first + (1.0 - beta_one) * grad
    second_new = beta_two * second + (1.0 - beta_two) * grad * grad
    param_new = param - learn_rate * first_new / (jnp.sqrt(second_new) + adam_eps)
    return (param_new, first_new, second_new)


def kernel(
    n_blk, chunks,
    data_hbm, mask_ref, u_hbm, um_hbm, uv_hbm, h_hbm, hm_hbm, hv_hbm,
    u_out, h_out,
    data, u, um, uv, ub, err, h, hm, hv, hn, hb, part, px, gb, gr, mx, h2, ho,
    in_sem, data_sem, out_sem, ho_sem,
    x_send, x_recv, h_send, h_recv, f_send, f_recv, g_send, g_recv,
    m_send, m_recv, o_send, o_recv, p_send, p_recv, q_send, q_recv,
):
    systems = u.shape[0]
    count = len(chunks)
    last = count - 1
    me = lax.axis_index("blk")
    core = lax.axis_index("rep")
    other = 1 - core
    after, before = lax.rem(me + 1, n_blk), lax.rem(me + n_blk - 1, n_blk)
    after2, before2 = lax.rem(me + 2, n_blk), lax.rem(me + n_blk - 2, n_blk)

    barrier = pltpu.get_barrier_semaphore()
    friends = [
        {"rep": other},
        {"blk": after}, {"blk": after, "rep": other},
        {"blk": before}, {"blk": before, "rep": other},
        {"blk": after2}, {"blk": before2},
    ]
    for friend in friends:
        pl.semaphore_signal(barrier, inc=1, device_id=friend, device_id_type=MESH)

    def fetch(src, dst, k):
        return pltpu.make_async_copy(src, dst, in_sem.at[k])

    in_h, in_u = fetch(h_hbm, h, 0), fetch(u_hbm, u, 1)
    in_hm, in_hv = fetch(hm_hbm, hm, 2), fetch(hv_hbm, hv, 3)
    in_um, in_uv = fetch(um_hbm, um, 4), fetch(uv_hbm, uv, 5)
    in_data = [
        [
            pltpu.make_async_copy(
                data_hbm.at[s, :, pl.ds(off, w)], data.at[s, :, pl.ds(off, w)], data_sem.at[s, c]
            )
            for c, (off, w) in enumerate(chunks)
        ]
        for s in range(2)
    ]
    in_h.start()
    in_u.start()
    for c in range(count):
        in_data[0][c].start()
        if c == 0:
            in_hm.start()
            in_hv.start()
    in_um.start()
    in_uv.start()
    for c in range(count):
        in_data[1][c].start()

    def remote(src, dst, send, recv, device):
        return pltpu.make_async_remote_copy(
            src_ref=src, dst_ref=dst, send_sem=send, recv_sem=recv,
            device_id=device, device_id_type=MESH,
        )

    def rows_of(c, which):
        off, w = chunks[c]
        return pl.ds(pl.multiple_of(off + which * (w // 2), w // 2), w // 2)

    def half_of(c):
        off, w = chunks[c]
        return pl.ds(off // 2, w // 2)

    swap = [
        [
            remote(part.at[s, rows_of(c, other)], px.at[s, half_of(c)],
                   x_send.at[s, c], x_recv.at[s, c], {"rep": other})
            for c in range(count)
        ]
        for s in range(2)
    ]
    pass_h = [
        remote(h.at[rows_of(c, core)], hn.at[rows_of(c, core)], h_send.at[c], h_recv.at[c], {"blk": after})
        for c in range(count)
    ]
    share_h = [
        remote(hn.at[rows_of(c, core)], hn.at[rows_of(c, core)], f_send.at[c], f_recv.at[c], {"rep": other})
        for c in range(count)
    ]
    back = [
        remote(gb.at[half_of(c)], gr.at[half_of(c)], g_send.at[c], g_recv.at[c], {"blk": before})
        for c in range(count)
    ]
    final = [
        remote(h2.at[half_of(c)], (h_out if c == last else ho).at[rows_of(c, core)], o_send.at[c], o_recv.at[c],
               {"blk": after2 if c in HOME else after})
        for c in range(count)
    ]
    share_out = [
        remote(ho.at[rows_of(c, core)], h_out.at[rows_of(c, core)], p_send.at[c], p_recv.at[c], {"rep": other})
        for c in range(last)
    ]
    final_two = remote(
        h2.at[half_of(last)], h_out.at[rows_of(last, core)], q_send, q_recv, {"blk": after, "rep": other}
    )
    pass_m = [
        [
            remote(src.at[rows_of(c, core)], mx.at[k, half_of(c)], m_send.at[k, c], m_recv.at[k, c], {"blk": after})
            for k, src in enumerate((hm, hv))
        ]
        for c in range(count)
    ]
    travel = [c for c in range(count) if c not in HOME]

    def grads(s, c):
        off, w = chunks[c]

        def block(i):
            rows = pl.ds(pl.multiple_of(i * ROWS, ROWS), ROWS)
            predict = lax.dot_general(
                ub[rows, :], hb[off : off + w, :], (((1,), (1,)), ((), ())),
                preferred_element_type=jnp.float32,
            )
            diff = predict - data[s, rows, off : off + w].astype(jnp.float32)
            for a in range(ROWS // TILE):
                for b in range(w // TILE):
                    keep = mask_ref[off // TILE + b, s, i * (ROWS // TILE) + a].astype(jnp.float32)
                    piece = diff[a * TILE : (a + 1) * TILE, b * TILE : (b + 1) * TILE] * keep
                    err[
                        pl.ds(pl.multiple_of(i * ROWS + a * TILE, TILE), TILE),
                        off + b * TILE : off + (b + 1) * TILE,
                    ] = piece.astype(jnp.bfloat16)

        def pair(i, carry):
            block(2 * i)
            block(2 * i + 1)
            return carry

        lax.fori_loop(0, systems // ROWS // 2, pair, 0)
        part[s, off : off + w, :] = lax.dot_general(
            err[:, off : off + w], ub[...], (((0,), (0,)), ((), ())),
            preferred_element_type=jnp.float32,
        )

    def sys_block(s, i):
        rows = pl.ds(pl.multiple_of(i * ROWS, ROWS), ROWS)
        grad = jnp.dot(err[rows, :], hb[...], preferred_element_type=jnp.float32)
        param = u[rows, :]
        new, one, two = adam_step(param, um[rows, :], uv[rows, :], grad + decay_weight * param)
        u[rows, :] = new
        if s == 0:
            um[rows, :] = one
            uv[rows, :] = two
            ub[rows, :] = new.astype(jnp.bfloat16)

    pieces = 4
    per = systems // pieces

    def sys_piece(s, p):
        for i in range(p * per // ROWS, (p + 1) * per // ROWS):
            sys_block(s, i)

    out_copy = [
        pltpu.make_async_copy(u.at[pl.ds(p * per, per)], u_out.at[pl.ds(p * per, per)], out_sem.at[p])
        for p in range(pieces)
    ]

    ho_copy = [
        pltpu.make_async_copy(ho.at[rows_of(c, core)], h_out.at[rows_of(c, core)], ho_sem.at[c])
        for c in range(last)
    ]

    def home_first(c):
        swap[0][c].wait_recv()
        rows = rows_of(c, core)
        param = h[rows, :]
        grad = part[0, rows, :] + px[0, half_of(c), :] + decay_weight * param
        new, one, two = adam_step(param, hm[rows, :], hv[rows, :], grad)
        h[rows, :] = new
        hm[rows, :] = one
        hv[rows, :] = two
        pass_h[c].start()
        if c == last:
            for k in travel:
                for copy in pass_m[k]:
                    copy.start()

    def hand_on(c):
        pass_h[c].wait_recv()
        share_h[c].start()

    def give_back(c):
        swap[1][c].wait_recv()
        rows = rows_of(c, core)
        gb[half_of(c), :] = part[1, rows, :] + px[1, half_of(c), :]
        back[c].start()

    def home_second(c):
        back[c].wait_recv()
        rows = rows_of(c, core)
        param = h[rows, :]
        grad = gr[half_of(c), :] + decay_weight * param
        h2[half_of(c), :] = adam_step(param, hm[rows, :], hv[rows, :], grad)[0]
        final[c].start()

    def finish(c):
        for copy in pass_m[c]:
            copy.wait_recv()
        swap[1][c].wait_recv()
        rows = rows_of(c, core)
        param = hn[rows, :]
        grad = part[1, rows, :] + px[1, half_of(c), :] + decay_weight * param
        h2[half_of(c), :] = adam_step(param, mx[0, half_of(c), :], mx[1, half_of(c), :], grad)[0]
        final[c].start()
        if c == last:
            final_two.start()

    def share_final(c):
        final[c].wait_recv()
        share_out[c].start()
        ho_copy[c].start()

    in_h.wait()
    hb[...] = h[...].astype(jnp.bfloat16)
    in_u.wait()
    ub[...] = u[...].astype(jnp.bfloat16)
    for c in range(count):
        in_data[0][c].wait()
        grads(0, c)
        if c == 0:
            pl.semaphore_wait(barrier, len(friends))
            in_hm.wait()
            in_hv.wait()
        swap[0][c].start()
        if c >= 1:
            home_first(c - 1)
    in_um.wait()
    in_uv.wait()
    sys_piece(0, 0)
    home_first(last)
    for p in range(1, pieces):
        sys_piece(0, p)
    hand_on(0)

    for c, (off, w) in enumerate(chunks):
        if c < last:
            hand_on(c + 1)
        in_data[1][c].wait()
        share_h[c].wait_recv()
        hb[off : off + w, :] = hn[off : off + w, :].astype(jnp.bfloat16)
        grads(1, c)
        swap[1][c].start()
        if c >= 1:
            give_back(c - 1) if c - 1 in HOME else finish(c - 1)
    sys_piece(1, 0)
    out_copy[0].start()
    finish(last)
    for c in HOME:
        home_second(c)
    for p in range(1, pieces):
        sys_piece(1, p)
        out_copy[p].start()
    for c in range(last):
        share_final(c)

    for c in range(last):
        share_out[c].wait_recv()
    for s in range(2):
        for c in range(count):
            swap[s][c].wait_send()
    for group in (pass_h, share_h, final, share_out, [final_two]):
        for copy in group:
            copy.wait_send()
    for c in range(count):
        for copy in [back[c]] if c in HOME else pass_m[c]:
            copy.wait_send()
    final[last].wait_recv()
    final_two.wait_recv()
    for copy in out_copy + ho_copy:
        copy.wait()


def place_kernel(u_in, h_in, u_to, h_to, u_mid, h_mid, read_sem, write_sem):
    per = u_in.shape[0] // 4
    moves = [(h_in, h_mid, h_to, pl.ds(0, h_in.shape[0]))] + [
        (u_in, u_mid, u_to, pl.ds(k * per, per)) for k in range(4)
    ]
    reads = [
        pltpu.make_async_copy(src.at[rows], mid.at[rows], read_sem.at[k])
        for k, (src, mid, _, rows) in enumerate(moves)
    ]
    writes = [
        pltpu.make_async_copy(mid.at[rows], dst.at[rows], write_sem.at[k])
        for k, (_, mid, dst, rows) in enumerate(moves)
    ]
    for read in reads:
        read.start()
    for read, write in zip(reads, writes):
        read.wait()
        write.start()
    for write in writes:
        write.wait()


def placed(u, h):
    anywhere = pl.BlockSpec(memory_space=pl.ANY)
    return pl.pallas_call(
        place_kernel,
        out_shape=(jax.ShapeDtypeStruct(u.shape, u.dtype), jax.ShapeDtypeStruct(h.shape, h.dtype)),
        in_specs=[anywhere, anywhere],
        out_specs=(anywhere, anywhere),
        scratch_shapes=[
            pltpu.VMEM(u.shape, u.dtype), pltpu.VMEM(h.shape, h.dtype),
            pltpu.SemaphoreType.DMA((5,)), pltpu.SemaphoreType.DMA((5,)),
        ],
        compiler_params=pltpu.CompilerParams(vmem_limit_bytes=56 * 1024 * 1024),
    )(u, h)


def on_device(
    readings, tile_mask, sys_factors, sys_first, sys_second, time_factors, time_first, time_second
):
    n_blk = lax.axis_size("blk")
    systems, rank = sys_factors.shape
    times = time_factors.shape[0]
    chunks = tuple((off, min(CHUNK, times - off)) for off in range(0, times, CHUNK))
    count = len(chunks)
    f32, bf16 = jnp.float32, jnp.bfloat16
    dma = pltpu.SemaphoreType.DMA
    anywhere = pl.BlockSpec(memory_space=pl.ANY)
    results = pl.pallas_call(
        functools.partial(kernel, n_blk, chunks),
        out_shape=(
            jax.ShapeDtypeStruct((systems, rank), f32),
            jax.ShapeDtypeStruct((times, rank), f32),
        ),
        in_specs=[anywhere, pl.BlockSpec(memory_space=pltpu.SMEM)] + [anywhere] * 6,
        out_specs=(anywhere, anywhere),
        scratch_shapes=[
            pltpu.VMEM((2, systems, times), bf16),
            pltpu.VMEM((systems, rank), f32),
            pltpu.VMEM((systems, rank), f32),
            pltpu.VMEM((systems, rank), f32),
            pltpu.VMEM((systems, rank), bf16),
            pltpu.VMEM((systems, times), bf16),
            pltpu.VMEM((times, rank), f32),
            pltpu.VMEM((times, rank), f32),
            pltpu.VMEM((times, rank), f32),
            pltpu.VMEM((times, rank), f32),
            pltpu.VMEM((times, rank), bf16),
            pltpu.VMEM((2, times, rank), f32),
            pltpu.VMEM((2, times // 2, rank), f32),
            pltpu.VMEM((times // 2, rank), f32),
            pltpu.VMEM((times // 2, rank), f32),
            pltpu.VMEM((2, times // 2, rank), f32),
            pltpu.VMEM((times // 2, rank), f32),
            pltpu.VMEM((times, rank), f32),
            dma((6,)), dma((2, count)), dma((4,)), dma((count,)),
            dma((2, count)), dma((2, count)),
            dma((count,)), dma((count,)),
            dma((count,)), dma((count,)),
            dma((count,)), dma((count,)),
            dma((2, count)), dma((2, count)),
            dma((count,)), dma((count,)),
            dma((count,)), dma((count,)),
            dma, dma,
        ],
        compiler_params=pltpu.CompilerParams(
            collective_id=0, has_side_effects=True, vmem_limit_bytes=56 * 1024 * 1024
        ),
    )(readings, jnp.transpose(tile_mask, (2, 0, 1)), sys_factors, sys_first, sys_second, time_factors, time_first, time_second)
    return placed(*results)


def solution(mesh):
    return jax.shard_map(
        on_device,
        mesh=mesh,
        in_specs=(
            P(None, ("region", "blk", "rep"), None),
            P(None, ("region", "blk", "rep"), None),
            P(("region", "blk", "rep"), None),
            P(("region", "blk", "rep"), None),
            P(("region", "blk", "rep"), None),
            P(("region", "blk"), None),
            P(("region", "blk"), None),
            P(("region", "blk"), None),
        ),
        out_specs=(P(("region", "blk", "rep"), None), P(("region", "blk"), None)),
        check_vma=False,
    )
```
